32 devices in a mesh: tm: 8 (over z, x), sx: 2 (over core), sy: 2 (over y).
Axes of the slice: x: 2, y: 2, z: 4, core: 2. Of those that a mesh axis runs over, the one named last changes fastest.
Arguments:
- initial_states: float32 [8, 8, 64, 256], P('tm', None, 'sx', 'sy'), may hold values from -6 to 6
- coarse_decay: float32 [8, 8, 64, 256], P('tm', None, 'sx', 'sy'), may hold values from 0 to 1, as said below
- power_map: float32 [8, 64, 256], P(None, 'sx', 'sy'), may hold values from 0.5 to 2
- power_mask: int32 [8, 4, 8], P('tm'), may hold values 0 or 1
- region_ids: int32 [8, 8], replicated, may hold values from 0 to 3
- region_conductivity: float32 [4], replicated, may hold values from 0.4 to 2.5
Outputs:
- cycle_states: float32 [8, 8, 64, 256], P('tm', None, 'sx', 'sy')
- jump_field: float32 [8, 8, 64, 256], P('tm', None, 'sx', 'sy')
The draws below stay inside these ranges and needn't reach their ends.
Inputs may be any that keep to these rules, and one draw needn't show every extreme that they name: `coarse_decay`: every entry lies between 0 and 1, and for every cell the product of its 8 factors is at most one half.
All inputs are finite; a program needn't handle non-finite values. No bound on the sum of `power_mask` on one device may be relied on, other than what follows from the above.
Results may differ from the reference program's by a relative error of at most 0.0001.
Values sent between devices are 32-bit elements; how exact they have to be, the bound alone decides.
A program may use at most 128 MiB of HBM per device.

```python
import math
import jax
import jax.numpy as jnp
from jax import lax

LAYERS = 8
RB = 8
REGIONS = 4
FSTEPS = 4
SWEEPS = 3
ITERS = 2
TIME_SLABS = 8
NX = 64
NY = 256
ROWBLOCKS = 8


def draw_coarse_decay(key, part):
    key_pick, key_fast, key_slow, key_strike_points, key_split_points = jax.random.split(key, 5)
    array_extent = (TIME_SLABS, LAYERS, NX, NY)
    share = 0.5
    slow_cells = jax.random.uniform(key_pick, (1, LAYERS, NX, NY), jnp.float32) < share
    fast_rate = jnp.exp(jax.random.uniform(key_fast, array_extent, jnp.float32, jnp.log(0.02), jnp.log(0.5)))
    slow_power = jax.random.uniform(key_slow, array_extent, jnp.float32, 0.32, 1.0)
    gradual_decline = jnp.exp(jnp.log(0.1) * slow_power / TIME_SLABS)
    pulse_strikes = jax.random.uniform(key_strike_points, array_extent, jnp.float32) < 3.0 / TIME_SLABS
    pulse_splits = jax.random.uniform(key_split_points, array_extent, jnp.float32, 0.5, 0.8)
    gradual_decline = jnp.where(pulse_strikes, gradual_decline * pulse_splits, gradual_decline)
    return jnp.where(slow_cells, gradual_decline, fast_rate).astype(jnp.float32)


def touch_ends(array, key, smallest, top_value):
    spot = [jax.random.randint(jax.random.fold_in(key, axis), (), 0, length) for axis, length in enumerate(array.shape)]
    longest = array.shape.index(max(array.shape))
    beside = spot[:longest] + [(spot[longest] + 1) % array.shape[longest]] + spot[longest + 1:]
    return array.at[tuple(spot)].set(smallest).at[tuple(beside)].set(top_value)


def level_of(stream_key, extent, cuts, low, largest):
    level, own = 1.0, jax.random.fold_in(stream_key, 6)
    for position, parts in cuts:
        steps = jnp.exp(jax.random.uniform(jax.random.fold_in(own, position), (parts,), jnp.float32, low / len(cuts), largest / len(cuts)))
        level = level * jnp.repeat(steps, extent[position] // parts).reshape([-1 if axis == position else 1 for axis in range(len(extent))])
    return level


def noise(key, extent, deviation, bound, cuts=(), kind=jnp.bfloat16):
    values = deviation * jax.random.normal(key, extent, jnp.float32)
    if cuts:
        values = values * level_of(key, extent, cuts, -0.22, 0.18)
    return jnp.clip(values, -bound, bound).astype(kind)


def setup_inputs(seed: int = 0) -> dict:
    keys = jax.random.split(jax.random.key(seed), 7)
    return {
        "initial_states": noise(keys[0], (TIME_SLABS, LAYERS, NX, NY), 1.0, 6.0, ((0, 8), (2, 2), (3, 2)), jnp.float32),
        "coarse_decay": draw_coarse_decay(jax.random.fold_in(keys[6], 71), 0),
        "power_map": jnp.clip(jnp.exp(math.log(2.0) - 1.3862944 * jax.random.uniform(keys[2], (LAYERS, NX, NY), jnp.float32) ** level_of(keys[2], (LAYERS, NX, NY), ((1, 2), (2, 2)), -0.2, 0.2)), 0.5, 2.0),
        "power_mask": touch_ends((jax.random.randint(keys[3], (TIME_SLABS, FSTEPS, ROWBLOCKS), 0, 2) < 1).astype(jnp.int32), jax.random.fold_in(keys[3], 1), 0, 1),
        "region_ids": touch_ends(jax.random.randint(keys[4], (LAYERS, ROWBLOCKS), 0, REGIONS), jax.random.fold_in(keys[4], 1), 0, REGIONS - 1).astype(jnp.int32),
        "region_conductivity": jnp.clip(jnp.exp(jax.random.uniform(keys[5], (REGIONS,), jnp.float32, math.log(0.4), math.log(2.5))), 0.4, 2.5),
    }


grid_xy = 1.0
grid_z = 0.5
sink_gain = 0.5
source_gain = 0.5
cond_slope = 0.25
joule_slope = 0.3


def base_rows(region_ids, region_conductivity):
    labels = jnp.arange(REGIONS, dtype=jnp.int32)
    chosen = (region_ids[:, :, None] == labels[None, None, :]).astype(jnp.float32)
    return jnp.sum(chosen * region_conductivity[None, None, :], axis=2)


def face_weights(cond_pad, weight_scale):
    middle = cond_pad[:, 1:-1, 1:-1]
    layer_index = lax.broadcasted_iota(jnp.int32, middle.shape, 0)
    blank_layer = jnp.zeros_like(middle[:1])
    layer_above = jnp.concatenate([middle[1:], blank_layer], axis=0)
    layer_below = jnp.concatenate([blank_layer, middle[:-1]], axis=0)
    weight_west = weight_scale * (grid_xy * (0.5 * (middle + cond_pad[:, :-2, 1:-1])))
    weight_east = weight_scale * (grid_xy * (0.5 * (middle + cond_pad[:, 2:, 1:-1])))
    weight_south = weight_scale * (grid_xy * (0.5 * (middle + cond_pad[:, 1:-1, :-2])))
    weight_north = weight_scale * (grid_xy * (0.5 * (middle + cond_pad[:, 1:-1, 2:])))
    weight_up = jnp.where(layer_index == middle.shape[0] - 1, jnp.zeros_like(middle), weight_scale * (grid_z * (0.5 * (middle + layer_above))))
    weight_down = jnp.where(layer_index == 0, weight_scale * (sink_gain * middle), weight_scale * (grid_z * (0.5 * (middle + layer_below))))
    denominator = 1.0 + (((((weight_west + weight_east) + weight_south) + weight_north) + weight_down) + weight_up)
    return (weight_west, weight_east, weight_south, weight_north, weight_down, weight_up), denominator


def relax(padded, weights, right_side, denominator):
    weight_west, weight_east, weight_south, weight_north, weight_down, weight_up = weights
    middle = padded[:, 1:-1, 1:-1]
    blank_layer = jnp.zeros_like(middle[:1])
    layer_above = jnp.concatenate([middle[1:], blank_layer], axis=0)
    layer_below = jnp.concatenate([blank_layer, middle[:-1]], axis=0)
    summed = weight_west * padded[:, :-2, 1:-1] + weight_east * padded[:, 2:, 1:-1]
    summed = summed + weight_south * padded[:, 1:-1, :-2] + weight_north * padded[:, 1:-1, 2:]
    summed = summed + weight_down * layer_below + weight_up * layer_above
    return (right_side + summed) / denominator


def fine_slab(initial, mask_rows, base_cond, power_map):
    current = initial
    previous = initial
    for substep in range(FSTEPS):
        if substep == 0:
            coef_now, coef_old, weight_scale = 1.0, 0.0, 1.0
        else:
            coef_now, coef_old, weight_scale = 4.0 / 3.0, -1.0 / 3.0, 2.0 / 3.0
        conductance = base_cond[:, :, None] * (1.0 - cond_slope * jnp.tanh(current))
        cond_pad = jnp.pad(conductance, ((0, 0), (1, 1), (1, 1)))
        weights, denominator = face_weights(cond_pad, weight_scale)
        heat_source = source_gain * mask_rows[substep][None, :, None] * power_map * (1.0 + joule_slope * jnp.tanh(current))
        right_side = coef_now * current + coef_old * previous + weight_scale * heat_source
        iterate = current
        for sweep_index in range(SWEEPS):
            iterate = relax(jnp.pad(iterate, ((0, 0), (1, 1), (1, 1))), weights, right_side, denominator)
        previous = current
        current = iterate
    return current


def periodic_solve(decay_rate, offset):
    def advance(running, slab_item):
        scale_sum, shift_sum = running
        rate_now, offset_now = slab_item
        return (scale_sum * rate_now, rate_now * shift_sum + offset_now), (scale_sum, shift_sum)

    unit_map = jnp.ones(decay_rate.shape[1:], jnp.float32)
    zero_map = jnp.zeros(decay_rate.shape[1:], jnp.float32)
    totals, prefixes = lax.scan(advance, (unit_map, zero_map), (decay_rate, offset))
    scale_total, shift_total = totals
    scale_pre, shift_pre = prefixes
    first_state = shift_total / (1.0 - scale_total)
    return scale_pre * first_state[None] + shift_pre


def reference(initial_states, coarse_decay, power_map, power_mask, region_ids, region_conductivity):
    base_cond = jnp.repeat(base_rows(region_ids, region_conductivity), RB, axis=1)
    mask_rows = jnp.repeat(power_mask.astype(jnp.float32), RB, axis=2)

    def fine_all(states):
        return lax.map(lambda bundle: fine_slab(bundle[0], bundle[1], base_cond, power_map), (states, mask_rows))

    states = initial_states
    jump_field = jnp.zeros_like(initial_states)
    for round_index in range(ITERS):
        fine_end = fine_all(states)
        if round_index == ITERS - 1:
            jump_field = fine_end - jnp.roll(states, -1, axis=0)
        offset = fine_end - coarse_decay * states
        states = periodic_solve(coarse_decay, offset)
    return states, jump_field
```

```python
import functools

import jax
import jax.numpy as jnp
from jax import lax
from jax.experimental import pallas as pl
from jax.experimental.pallas import tpu as pltpu
from jax.sharding import PartitionSpec as P

RB = 8
FSTEPS = 4
SWEEPS = 3
ITERS = 2
LAYERS = 8
ROWS = 32
COLS = 128
HALO = FSTEPS * SWEEPS
EXT = ROWS + HALO
PAD = 48
STRIP = 16
BLOCK = 4

cond_slope = 0.25
joule_slope = 0.3
MESH = pl.DeviceIdType.MESH


def kernel(
    slabs, solvers, chunk,
    state_ref, decay_ref, power_ref, mask_ref, ids_ref, cond_ref,
    out_ref, jump_ref,
    own, dec, off, packed, rows_in, side_in, corner_in,
    v, cond, rhs, wx, wy, wz, rden, power, base,
    a_in, b_in, u_out, u_in,
    near_send, near_recv, far_send, far_recv,
):
    tm, sx, sy = lax.axis_index("tm"), lax.axis_index("sx"), lax.axis_index("sy")
    other_core, side, corner = (tm, 1 - sx, sy), (tm, sx, 1 - sy), (tm, 1 - sx, 1 - sy)

    def slab_at(distance):
        return lax.rem(tm + distance, slabs)

    barrier = pltpu.get_barrier_semaphore()
    for peer in (other_core, side, corner):
        pl.semaphore_signal(barrier, inc=1, device_id=peer, device_id_type=MESH)
    for d in range(1, slabs):
        pl.semaphore_signal(barrier, inc=1, device_id=(slab_at(d), sx, sy), device_id_type=MESH)

    def grid_row(r):
        return r + sx * (ROWS - 1 - 2 * r)

    def grid_block(i):
        return i + sx * (ids_ref.shape[1] - 1 - 2 * i)

    lane = lax.broadcasted_iota(jnp.int32, (LAYERS, COLS), 1)
    window = lax.rem(lane // STRIP + 8, 8)
    edge_window = 7 * (1 - sy)

    def pack(slot, kind):
        for g in range(ROWS // 8):
            total = own[kind, 8 * g] if slot is None else u_in[slot, 8 * g]
            for i in range(1, 8):
                row = own[kind, 8 * g + i] if slot is None else u_in[slot, 8 * g + i]
                here = lax.rem(window - i + 8, 8) == edge_window
                total = jnp.where(here, pltpu.roll(row, STRIP * i, 1), total)
            packed[kind if slot is None else 2, g] = total

    def load_rows(r, carry):
        at = pl.ds(grid_row(r), LAYERS, ROWS)
        own[0, r] = state_ref[at, :]
        own[1, r] = power_ref[at, :]
        dec[r] = decay_ref[at, :]
        return carry

    lax.fori_loop(0, ROWS, load_rows, 0, unroll=True)
    pack(None, 0)
    pack(None, 1)

    pl.semaphore_wait(barrier, 3 + slabs - 1)

    def near(src_rows, src_strip, src_corner, slots, k):
        copies = [
            pltpu.make_async_remote_copy(
                src_ref=src, dst_ref=dst, send_sem=near_send.at[k + i], recv_sem=near_recv.at[k + i],
                device_id=peer, device_id_type=MESH,
            )
            for i, (src, dst, peer) in enumerate((
                (src_corner, corner_in.at[slots], corner),
                (src_strip, side_in.at[slots], side),
                (src_rows, rows_in.at[slots], other_core),
            ))
        ]
        for copy in copies:
            copy.start()
        return copies

    first = near(
        own.at[:, pl.ds(ROWS - HALO, HALO)], packed.at[pl.ds(0, 2)],
        packed.at[pl.ds(0, 2), pl.ds(2, 2)], pl.ds(0, 2), 0,
    )

    def to_solvers(src, dst, kind):
        def copy_at(d):
            target = slab_at(d)
            return pltpu.make_async_remote_copy(
                src_ref=src.at[pl.ds(target * chunk, chunk)], dst_ref=dst.at[tm],
                send_sem=far_send.at[kind, d], recv_sem=far_recv.at[kind, d],
                device_id=(target, sx, sy), device_id_type=MESH,
            )

        for d in range(1, slabs):
            guarded(slab_at(d) < solvers, copy_at(d).start)

        def keep():
            dst[tm] = src[pl.ds(tm * chunk, chunk)]

        guarded(tm < solvers, keep)

        def sent():
            for d in range(1, slabs):
                guarded(slab_at(d) < solvers, copy_at(d).wait_send)

        def arrived():
            for d in range(1, slabs):
                copy_at(d).wait_recv()

        return sent, arrived

    def guarded(condition, action):
        if solvers == slabs:
            action()
        else:
            pl.when(condition)(action)

    decay_sent, decay_arrived = to_solvers(dec, a_in, 0)

    blank = jnp.zeros((BLOCK, LAYERS, 2 * COLS), jnp.float32)

    def clear(i, carry):
        at = pl.ds(BLOCK * i, BLOCK)
        for slot in range(3):
            v[slot, at] = blank
        for ref in (cond, rhs, wx, wy, wz, rden, power):
            ref[at] = blank
        return carry

    lax.fori_loop(0, PAD // BLOCK, clear, 0, unroll=True)

    layer = lax.broadcasted_iota(jnp.int32, (LAYERS, 2 * COLS), 0)
    place = lax.broadcasted_iota(jnp.int32, (LAYERS, 2 * COLS), 1)
    for i in range(-(-EXT // RB)):
        block = grid_block(i)
        value = jnp.zeros((LAYERS, 2 * COLS), jnp.float32)
        for l in range(LAYERS):
            value = jnp.where(layer == l, cond_ref[ids_ref[l, block]], value)
        base[i] = value
    first_col = place == sy * COLS
    last_col = place == 2 * COLS - 1 - sy * COLS
    wy_mask = jnp.where(first_col, 0.0, 1.0)
    wz_mask = jnp.where(layer == 0, 0.0, 0.5)
    border = (
        jnp.where(layer == 0, 1.0, 0.0)
        + jnp.where(first_col, 1.0, 0.0)
        + jnp.where(last_col, 1.0, 0.0)
    )

    def spread(store, slot):
        for i in range(HALO):
            store(EXT - 1 - i, 0, rows_in[slot, i])
        for i in range(8):
            for g in range(ROWS // 8):
                store(8 * g + i, 1, pltpu.roll(side_in[slot, g], (COLS - STRIP * i) % COLS, 1))
            for g in range(2):
                r = 2 * ROWS - 1 - (16 + 8 * g + i)
                if r < EXT:
                    store(r, 1, pltpu.roll(corner_in[slot, g], (COLS - STRIP * i) % COLS, 1))

    def store_state(r, half, value):
        v[0, 1 + r, :, half * COLS:(half + 1) * COLS] = value

    def store_power(r, half, value):
        power[1 + r, :, half * COLS:(half + 1) * COLS] = value

    def sweep(source, target, count, with_weights):
        def body(i, carry):
            r = BLOCK * i
            at, before, after = pl.ds(r + 1, BLOCK), pl.ds(r, BLOCK), pl.ds(r + 2, BLOCK)
            if with_weights:
                k = cond[at]
                west = k + cond[before]
                east = k + cond[after]
                south = wy_mask * (k + pltpu.roll(k, 1, 2))
                down = wz_mask * (k + pltpu.roll(k, 1, 1))
                den = 1.0 + (
                    west + east + south + pltpu.roll(south, 2 * COLS - 1, 2)
                    + down + pltpu.roll(down, LAYERS - 1, 1) + border * k
                )
                inverse = 1.0 / den
                wx[at] = west
                wy[at] = south
                wz[at] = down
                rden[at] = inverse
            else:
                west, east, south, down, inverse = wx[at], wx[after], wy[at], wz[at], rden[at]
            mid = v[source, at]
            total = rhs[at] + west * v[source, before] + east * v[source, after]
            total = total + south * pltpu.roll(mid, 1, 2)
            total = total + pltpu.roll(south * mid, 2 * COLS - 1, 2)
            total = total + down * pltpu.roll(mid, 1, 1)
            total = total + pltpu.roll(down * mid, LAYERS - 1, 1)
            v[target, at] = total * inverse
            return carry

        lax.fori_loop(0, -(-count // BLOCK), body, 0, unroll=True)

    def fine():
        now, old, spare = 0, 1, 2
        for m in range(FSTEPS):
            coef_now, coef_old, scale = (1.0, 0.0, 1.0) if m == 0 else (4.0 / 3.0, -1.0 / 3.0, 2.0 / 3.0)
            half = 0.5 * scale
            reach = EXT - SWEEPS * m

            def prepare(i, carry, m=m, now=now, old=old, coef_now=coef_now, coef_old=coef_old, half=half):
                at = pl.ds(BLOCK * i + 1, BLOCK)
                block = (BLOCK * i) // RB
                current = v[now, at]
                t = jnp.tanh(current)
                cond[at] = base[block] * (half - (half * cond_slope) * t)
                on = half * mask_ref[0, m, grid_block(block)].astype(jnp.float32)
                total = (on * power[at]) * (1.0 + joule_slope * t)
                if m == 0:
                    total = total + current
                else:
                    total = total + (coef_now * current + coef_old * v[old, at])
                rhs[at] = total
                return carry

            lax.fori_loop(0, -(-reach // BLOCK), prepare, 0, unroll=True)
            sweep(now, spare, reach - 1, True)
            sweep(spare, old, reach - 2, False)
            sweep(old, spare, reach - 3, False)
            now, old, spare = spare, now, old
        return now

    def solve(it):
        a = [a_in[n] for n in range(slabs)]
        total = b_in[it, 0]
        product = a[0]
        for n in range(1, slabs):
            total = a[n] * total + b_in[it, n]
            product = product * a[n]
        state = total / (1.0 - product)
        for n in range(slabs):
            u_out[it, n] = state
            if n < slabs - 1:
                state = a[n] * state + b_in[it, n]

    def from_solvers(it):
        kind = 1 + ITERS + it

        def copy_at(d):
            target = slab_at(d)
            return pltpu.make_async_remote_copy(
                src_ref=u_out.at[it, target], dst_ref=u_in.at[it, pl.ds(tm * chunk, chunk)],
                send_sem=far_send.at[kind, d], recv_sem=far_recv.at[kind, d],
                device_id=(target, sx, sy), device_id_type=MESH,
            )

        def work():
            solve(it)
            for d in range(1, slabs):
                copy_at(d).start()
            u_in[it, pl.ds(tm * chunk, chunk)] = u_out[it, tm]

        guarded(tm < solvers, work)

        def sent():
            for d in range(1, slabs):
                copy_at(d).wait_send()

        def arrived():
            for d in range(1, slabs):
                guarded(lax.rem(tm - d + slabs, slabs) < solvers, copy_at(d).wait_recv)

        return lambda: guarded(tm < solvers, sent), arrived

    pending = [decay_sent]
    for r in range(ROWS):
        store_state(r, 0, own[0, r])
        store_power(r, 0, own[1, r])
    for copy in first:
        copy.wait_recv()
    pending += [copy.wait_send for copy in first]
    spread(store_state, 0)
    spread(store_power, 1)

    for it in range(ITERS):
        if it:
            for r in range(ROWS):
                store_state(r, 0, u_in[it - 1, r])
            pack(it - 1, 0)
            again = near(
                u_in.at[pl.ds(it - 1, 1), pl.ds(ROWS - HALO, HALO)], packed.at[pl.ds(2, 1)],
                packed.at[pl.ds(2, 1), pl.ds(2, 2)], pl.ds(2, 1), 3,
            )
            for copy in again:
                copy.wait_recv()
            pending += [copy.wait_send for copy in again]
            spread(store_state, 2)
        end = fine()

        def offsets(i, carry, it=it, end=end):
            at = pl.ds(BLOCK * i, BLOCK)
            start = own[0, at] if it == 0 else u_in[it - 1, at]
            off[it, at] = v[end, pl.ds(BLOCK * i + 1, BLOCK), :, 0:COLS] - dec[at] * start
            return carry

        lax.fori_loop(0, ROWS // BLOCK, offsets, 0, unroll=True)
        sent, arrived = to_solvers(off.at[it], b_in.at[it], 1 + it)
        pending.append(sent)
        if it == 0:
            guarded(tm < solvers, decay_arrived)
        if it == ITERS - 1:

            def jumps(r, carry, it=it, end=end):
                following = dec[r] * u_in[it - 1, r] + off[it - 1, r]
                jump_ref[pl.ds(grid_row(r), LAYERS, ROWS), :] = v[end, r + 1, :, 0:COLS] - following
                return carry

            lax.fori_loop(0, ROWS, jumps, 0, unroll=True)
        guarded(tm < solvers, arrived)
        sent, arrived = from_solvers(it)
        pending.append(sent)
        arrived()

    def finish(r, carry):
        out_ref[pl.ds(grid_row(r), LAYERS, ROWS), :] = u_in[ITERS - 1, r]
        return carry

    lax.fori_loop(0, ROWS, finish, 0, unroll=True)
    for wait in pending:
        wait()


def shards(slabs, initial_states, coarse_decay, power_map, power_mask, region_ids, region_conductivity):
    solvers = min(slabs, ROWS)
    chunk = ROWS // solvers
    flat = (LAYERS * ROWS, COLS)
    f32 = jnp.float32
    tile = (ROWS, LAYERS, COLS)
    wide = (PAD, LAYERS, 2 * COLS)
    vmem = pl.BlockSpec(memory_space=pltpu.VMEM)
    smem = pl.BlockSpec(memory_space=pltpu.SMEM)
    kinds = 1 + 2 * ITERS
    states, jump = pl.pallas_call(
        functools.partial(kernel, slabs, solvers, chunk),
        out_shape=[jax.ShapeDtypeStruct(flat, f32)] * 2,
        in_specs=[vmem] * 3 + [smem] * 3,
        out_specs=[vmem] * 2,
        scratch_shapes=[
            pltpu.VMEM((2,) + tile, f32),
            pltpu.VMEM(tile, f32),
            pltpu.VMEM((ITERS,) + tile, f32),
            pltpu.VMEM((3, ROWS // 8, LAYERS, COLS), f32),
            pltpu.VMEM((3, HALO, LAYERS, COLS), f32),
            pltpu.VMEM((3, ROWS // 8, LAYERS, COLS), f32),
            pltpu.VMEM((3, 2, LAYERS, COLS), f32),
            pltpu.VMEM((3,) + wide, f32),
            *[pltpu.VMEM(wide, f32) for _ in range(7)],
            pltpu.VMEM((-(-EXT // RB), LAYERS, 2 * COLS), f32),
            pltpu.VMEM((slabs, chunk, LAYERS, COLS), f32),
            pltpu.VMEM((ITERS, slabs, chunk, LAYERS, COLS), f32),
            pltpu.VMEM((ITERS, slabs, chunk, LAYERS, COLS), f32),
            pltpu.VMEM((ITERS,) + tile, f32),
            pltpu.SemaphoreType.DMA((6,)),
            pltpu.SemaphoreType.DMA((6,)),
            pltpu.SemaphoreType.DMA((kinds, slabs)),
            pltpu.SemaphoreType.DMA((kinds, slabs)),
        ],
        compiler_params=pltpu.CompilerParams(
            collective_id=0, has_side_effects=True, vmem_limit_bytes=24 * 2**20
        ),
    )(
        initial_states.reshape(flat), coarse_decay.reshape(flat), power_map.reshape(flat),
        power_mask, region_ids, region_conductivity,
    )
    return states.reshape(initial_states.shape), jump.reshape(initial_states.shape)


def solution(mesh):
    return jax.shard_map(
        functools.partial(shards, mesh.shape["tm"]),
        mesh=mesh,
        in_specs=(
            P("tm", None, "sx", "sy"),
            P("tm", None, "sx", "sy"),
            P(None, "sx", "sy"),
            P("tm", None, None),
            P(),
            P(),
        ),
        out_specs=(P("tm", None, "sx", "sy"), P("tm", None, "sx", "sy")),
        check_vma=False,
    )
```

```python
import functools

import jax
import jax.numpy as jnp
from jax import lax
from jax.experimental import pallas as pl
from jax.experimental.pallas import tpu as pltpu
from jax.sharding import PartitionSpec as P

RB = 8
FSTEPS = 4
SWEEPS = 3
ITERS = 2
LAYERS = 8
ROWS = 32
COLS = 128
HALO = FSTEPS * SWEEPS
EXT = ROWS + HALO
STRIP = 16
BLOCK = 4

cond_slope = 0.25
joule_slope = 0.3
MESH = pl.DeviceIdType.MESH


def kernel(
    slabs, solvers, chunk,
    state_hbm, decay_hbm, power_hbm, mask_hbm, ids_hbm, cond_hbm,
    out_ref, jump_ref,
    state_ref, decay_ref, power_ref, mask_ref, ids_ref, cond_ref, load_sem,
    own, dec, off, packed, rows_in, side_in, corner_in,
    v, cond, rhs, wx, wy, wz, rden, power, base,
    a_in, b_in, u_out, u_in,
    near_send, near_recv, far_send, far_recv,
):
    tm, sx, sy = lax.axis_index("tm"), lax.axis_index("sx"), lax.axis_index("sy")
    other_core, side, corner = (tm, 1 - sx, sy), (tm, sx, 1 - sy), (tm, 1 - sx, 1 - sy)

    loads = [
        pltpu.make_async_copy(src, dst, load_sem.at[i])
        for i, (src, dst) in enumerate((
            (state_hbm, state_ref), (power_hbm, power_ref), (decay_hbm, decay_ref),
            (ids_hbm, ids_ref), (cond_hbm, cond_ref), (mask_hbm, mask_ref),
        ))
    ]
    for load in loads:
        load.start()

    def slab_at(distance):
        return lax.rem(tm + distance, slabs)

    barrier = pltpu.get_barrier_semaphore()
    for peer in (other_core, side, corner):
        pl.semaphore_signal(barrier, inc=1, device_id=peer, device_id_type=MESH)
    for d in range(1, slabs):
        pl.semaphore_signal(barrier, inc=1, device_id=(slab_at(d), sx, sy), device_id_type=MESH)

    def grid_row(r):
        return r + sx * (ROWS - 1 - 2 * r)

    def grid_block(i):
        return i + sx * (ids_ref.shape[1] - 1 - 2 * i)

    lane = lax.broadcasted_iota(jnp.int32, (LAYERS, COLS), 1)
    window = lax.rem(lane // STRIP + 8, 8)
    edge_window = 7 * (1 - sy)

    def pack(slot, kind):
        for g in range(ROWS // 8):
            total = own[kind, 8 * g] if slot is None else u_in[slot, 8 * g]
            for i in range(1, 8):
                row = own[kind, 8 * g + i] if slot is None else u_in[slot, 8 * g + i]
                here = lax.rem(window - i + 8, 8) == edge_window
                total = jnp.where(here, pltpu.roll(row, STRIP * i, 1), total)
            packed[kind if slot is None else 2, g] = total

    def load_rows(r, carry):
        at = pl.ds(grid_row(r), LAYERS, ROWS)
        own[0, r] = state_ref[at, :]
        own[1, r] = power_ref[at, :]
        dec[r] = decay_ref[at, :]
        return carry

    for load in loads:
        load.wait()
    lax.fori_loop(0, ROWS, load_rows, 0, unroll=True)
    pack(None, 0)
    pack(None, 1)

    pl.semaphore_wait(barrier, 3 + slabs - 1)

    def near(src_rows, src_strip, src_corner, slots, k):
        copies = [
            pltpu.make_async_remote_copy(
                src_ref=src, dst_ref=dst, send_sem=near_send.at[k + i], recv_sem=near_recv.at[k + i],
                device_id=peer, device_id_type=MESH,
            )
            for i, (src, dst, peer) in enumerate((
                (src_corner, corner_in.at[slots], corner),
                (src_strip, side_in.at[slots], side),
                (src_rows, rows_in.at[slots], other_core),
            ))
        ]
        for copy in copies:
            copy.start()
        return copies

    first = near(
        own.at[:, pl.ds(ROWS - HALO, HALO)], packed.at[pl.ds(0, 2)],
        packed.at[pl.ds(0, 2), pl.ds(2, 2)], pl.ds(0, 2), 0,
    )

    def chunk_of(t):
        return t // 2 + (solvers // 2) * lax.rem(t + t // 2, 2)

    def rows_of(t):
        return pl.ds(chunk_of(t) * chunk, chunk)

    def to_solvers(src, dst, kind):
        def copy_at(d):
            target = slab_at(d)
            return pltpu.make_async_remote_copy(
                src_ref=src.at[rows_of(target)], dst_ref=dst.at[tm],
                send_sem=far_send.at[kind, d], recv_sem=far_recv.at[kind, d],
                device_id=(target, sx, sy), device_id_type=MESH,
            )

        def send(half):
            for d in range(1, slabs):
                target = slab_at(d)
                mine = chunk_of(target) // (solvers // 2) == half
                pl.when(mine & (target < solvers))(copy_at(d).start)

        def keep():
            def store():
                dst[tm] = src[rows_of(tm)]

            guarded(tm < solvers, store)

        def sent():
            for d in range(1, slabs):
                guarded(slab_at(d) < solvers, copy_at(d).wait_send)

        def arrived():
            for d in range(1, slabs):
                copy_at(d).wait_recv()

        return send, keep, sent, arrived

    def guarded(condition, action):
        if solvers == slabs:
            action()
        else:
            pl.when(condition)(action)

    send, keep, decay_sent, decay_arrived = to_solvers(dec, a_in, 0)
    send(0)
    send(1)
    keep()

    blank = jnp.zeros((LAYERS, 2 * COLS), jnp.float32)
    for stage in range(HALO + 1):
        v[stage, 0] = blank
    for m in range(FSTEPS):
        cond[m, 0] = blank

    layer = lax.broadcasted_iota(jnp.int32, (LAYERS, 2 * COLS), 0)
    place = lax.broadcasted_iota(jnp.int32, (LAYERS, 2 * COLS), 1)
    for i in range(-(-EXT // RB)):
        block = grid_block(i)
        value = jnp.zeros((LAYERS, 2 * COLS), jnp.float32)
        for l in range(LAYERS):
            value = jnp.where(layer == l, cond_ref[ids_ref[l, block]], value)
        base[i] = value
    first_col = place == sy * COLS
    last_col = place == 2 * COLS - 1 - sy * COLS
    wy_mask = jnp.where(first_col, 0.0, 1.0)
    wz_mask = jnp.where(layer == 0, 0.0, 0.5)
    border = (
        jnp.where(layer == 0, 1.0, 0.0)
        + jnp.where(first_col, 1.0, 0.0)
        + jnp.where(last_col, 1.0, 0.0)
    )

    def spread_side(store, slot):
        for i in range(8):
            for g in range(ROWS // 8):
                store(8 * g + i, 1, pltpu.roll(side_in[slot, g], (COLS - STRIP * i) % COLS, 1))

    def spread_far(store, slot):
        for i in range(HALO):
            store(EXT - 1 - i, 0, rows_in[slot, i])
        for i in range(8):
            for g in range(2):
                r = 2 * ROWS - 1 - (16 + 8 * g + i)
                if r < EXT:
                    store(r, 1, pltpu.roll(corner_in[slot, g], (COLS - STRIP * i) % COLS, 1))

    def store_state(r, half, value):
        v[0, 1 + r, :, half * COLS:(half + 1) * COLS] = value

    def store_power(r, half, value):
        power[1 + r, :, half * COLS:(half + 1) * COLS] = value

    def over(first, last, body):
        full = (last - first) // BLOCK

        def step(i, carry):
            body(first + BLOCK * i, BLOCK)
            return carry

        lax.fori_loop(0, full, step, 0, unroll=True)
        if first + BLOCK * full < last:
            body(first + BLOCK * full, last - first - BLOCK * full)

    def sweep(m, index, first, last):
        source = SWEEPS * m + index

        def body(r, size):
            at, before, after = pl.ds(r + 1, size), pl.ds(r, size), pl.ds(r + 2, size)
            if index == 0:
                k = cond[m, at]
                west = k + cond[m, before]
                east = k + cond[m, after]
                south = wy_mask * (k + pltpu.roll(k, 1, 2))
                down = wz_mask * (k + pltpu.roll(k, 1, 1))
                den = 1.0 + (
                    west + east + south + pltpu.roll(south, 2 * COLS - 1, 2)
                    + down + pltpu.roll(down, LAYERS - 1, 1) + border * k
                )
                inverse = 1.0 / den
                wx[m, at] = west
                wy[m, at] = south
                wz[m, at] = down
                rden[m, at] = inverse
            else:
                west, east, south = wx[m, at], wx[m, after], wy[m, at]
                down, inverse = wz[m, at], rden[m, at]
            mid = v[source, at]
            total = rhs[m, at] + west * v[source, before] + east * v[source, after]
            total = total + south * pltpu.roll(mid, 1, 2)
            total = total + pltpu.roll(south * mid, 2 * COLS - 1, 2)
            total = total + down * pltpu.roll(mid, 1, 1)
            total = total + pltpu.roll(down * mid, LAYERS - 1, 1)
            v[source + 1, at] = total * inverse

        over(first, last, body)

    def prepare(m, first, last):
        coef_now, coef_old, scale = (1.0, 0.0, 1.0) if m == 0 else (4.0 / 3.0, -1.0 / 3.0, 2.0 / 3.0)
        half = 0.5 * scale
        now = SWEEPS * m

        def body(r, size):
            at = pl.ds(r + 1, size)
            block = r // RB
            current = v[now, at]
            t = jnp.tanh(current)
            cond[m, at] = base[block] * (half - (half * cond_slope) * t)
            on = half * mask_ref[0, m, grid_block(block)].astype(jnp.float32)
            total = (on * power[at]) * (1.0 + joule_slope * t)
            if m == 0:
                total = total + current
            else:
                total = total + (coef_now * current + coef_old * v[now - SWEEPS, at])
            rhs[m, at] = total

        aligned = min(-(-first // BLOCK) * BLOCK, last)
        if first < aligned:
            body(first, aligned - first)
        over(aligned, last, body)

    def fine(done, reached):
        for m in range(FSTEPS):
            left = SWEEPS * (FSTEPS - m)
            prepare(m, done + left if done else 0, reached + left)
            for index in range(SWEEPS):
                left -= 1
                sweep(m, index, done + left if done else 0, reached + left)

    def solve(it):
        a = [a_in[n] for n in range(slabs)]
        total = b_in[it, 0]
        product = a[0]
        for n in range(1, slabs):
            total = a[n] * total + b_in[it, n]
            product = product * a[n]
        state = total / (1.0 - product)
        for n in range(slabs):
            u_out[it, n] = state
            if n < slabs - 1:
                state = a[n] * state + b_in[it, n]

    def from_solvers(it):
        kind = 1 + ITERS + it

        def copy_at(d):
            target = slab_at(d)
            return pltpu.make_async_remote_copy(
                src_ref=u_out.at[it, target], dst_ref=u_in.at[it, rows_of(tm)],
                send_sem=far_send.at[kind, d], recv_sem=far_recv.at[kind, d],
                device_id=(target, sx, sy), device_id_type=MESH,
            )

        def work():
            solve(it)
            for d in range(1, slabs):
                copy_at(d).start()
            u_in[it, rows_of(tm)] = u_out[it, tm]

        guarded(tm < solvers, work)

        def sent():
            for d in range(1, slabs):
                copy_at(d).wait_send()

        def arrived():
            for d in range(1, slabs):
                guarded(lax.rem(tm - d + slabs, slabs) < solvers, copy_at(d).wait_recv)

        return lambda: guarded(tm < solvers, sent), arrived

    pending = [decay_sent]
    for r in range(ROWS):
        store_state(r, 0, own[0, r])
        store_power(r, 0, own[1, r])
    corner_copy, side_copy, rows_copy = first
    pending += [copy.wait_send for copy in first]
    side_copy.wait_recv()
    spread_side(store_state, 0)
    spread_side(store_power, 1)

    for it in range(ITERS):
        if it:
            pack(it - 1, 0)
            again = near(
                u_in.at[pl.ds(it - 1, 1), pl.ds(ROWS - HALO, HALO)], packed.at[pl.ds(2, 1)],
                packed.at[pl.ds(2, 1), pl.ds(2, 2)], pl.ds(2, 1), 3,
            )
            corner_copy, side_copy, rows_copy = again
            pending += [copy.wait_send for copy in again]
            for r in range(ROWS):
                store_state(r, 0, u_in[it - 1, r])
            side_copy.wait_recv()
            spread_side(store_state, 2)
        send, keep, sent, arrived = to_solvers(off.at[it], b_in.at[it], 1 + it)

        def offsets(r, size, it=it):
            at = pl.ds(r, size)
            start = own[0, at] if it == 0 else u_in[it - 1, at]
            off[it, at] = v[HALO, pl.ds(r + 1, size), :, 0:COLS] - dec[at] * start

        middle = ROWS // 2
        fine(0, middle)
        over(0, middle, offsets)
        send(0)
        rows_copy.wait_recv()
        corner_copy.wait_recv()
        spread_far(store_state, 2 if it else 0)
        if it == 0:
            spread_far(store_power, 1)
        fine(middle, ROWS)
        over(middle, ROWS, offsets)
        send(1)
        keep()
        pending.append(sent)
        if it == 0:
            guarded(tm < solvers, decay_arrived)
        if it == ITERS - 1:

            def jumps(r, carry, it=it):
                following = dec[r] * u_in[it - 1, r] + off[it - 1, r]
                jump_ref[pl.ds(grid_row(r), LAYERS, ROWS), :] = v[HALO, r + 1, :, 0:COLS] - following
                return carry

            lax.fori_loop(0, ROWS, jumps, 0, unroll=True)
        guarded(tm < solvers, arrived)
        sent, arrived = from_solvers(it)
        pending.append(sent)
        arrived()

    def finish(r, carry):
        out_ref[pl.ds(grid_row(r), LAYERS, ROWS), :] = u_in[ITERS - 1, r]
        return carry

    lax.fori_loop(0, ROWS, finish, 0, unroll=True)
    for wait in pending:
        wait()


def shards(slabs, initial_states, coarse_decay, power_map, power_mask, region_ids, region_conductivity):
    solvers = min(slabs, ROWS)
    chunk = ROWS // solvers
    flat = (LAYERS * ROWS, COLS)
    f32 = jnp.float32
    tile = (ROWS, LAYERS, COLS)
    wide = (EXT + 2, LAYERS, 2 * COLS)
    steps = (FSTEPS,) + wide
    vmem = pl.BlockSpec(memory_space=pltpu.VMEM)
    anywhere = pl.BlockSpec(memory_space=pl.ANY)
    kinds = 1 + 2 * ITERS
    states, jump = pl.pallas_call(
        functools.partial(kernel, slabs, solvers, chunk),
        out_shape=[jax.ShapeDtypeStruct(flat, f32)] * 2,
        in_specs=[anywhere] * 6,
        out_specs=[vmem] * 2,
        scratch_shapes=[
            *[pltpu.VMEM(flat, f32) for _ in range(3)],
            pltpu.SMEM(power_mask.shape, jnp.int32),
            pltpu.SMEM(region_ids.shape, jnp.int32),
            pltpu.SMEM(region_conductivity.shape, f32),
            pltpu.SemaphoreType.DMA((6,)),
            pltpu.VMEM((2,) + tile, f32),
            pltpu.VMEM(tile, f32),
            pltpu.VMEM((ITERS,) + tile, f32),
            pltpu.VMEM((3, ROWS // 8, LAYERS, COLS), f32),
            pltpu.VMEM((3, HALO, LAYERS, COLS), f32),
            pltpu.VMEM((3, ROWS // 8, LAYERS, COLS), f32),
            pltpu.VMEM((3, 2, LAYERS, COLS), f32),
            pltpu.VMEM((HALO + 1,) + wide, f32),
            *[pltpu.VMEM(steps, f32) for _ in range(6)],
            pltpu.VMEM(wide, f32),
            pltpu.VMEM((-(-EXT // RB), LAYERS, 2 * COLS), f32),
            pltpu.VMEM((slabs, chunk, LAYERS, COLS), f32),
            pltpu.VMEM((ITERS, slabs, chunk, LAYERS, COLS), f32),
            pltpu.VMEM((ITERS, slabs, chunk, LAYERS, COLS), f32),
            pltpu.VMEM((ITERS,) + tile, f32),
            pltpu.SemaphoreType.DMA((6,)),
            pltpu.SemaphoreType.DMA((6,)),
            pltpu.SemaphoreType.DMA((kinds, slabs)),
            pltpu.SemaphoreType.DMA((kinds, slabs)),
        ],
        compiler_params=pltpu.CompilerParams(
            collective_id=0, has_side_effects=True, vmem_limit_bytes=56 * 2**20
        ),
    )(
        initial_states.reshape(flat), coarse_decay.reshape(flat), power_map.reshape(flat),
        power_mask, region_ids, region_conductivity,
    )
    return states.reshape(initial_states.shape), jump.reshape(initial_states.shape)


def solution(mesh):
    return jax.shard_map(
        functools.partial(shards, mesh.shape["tm"]),
        mesh=mesh,
        in_specs=(
            P("tm", None, "sx", "sy"),
            P("tm", None, "sx", "sy"),
            P(None, "sx", "sy"),
            P("tm", None, None),
            P(),
            P(),
        ),
        out_specs=(P("tm", None, "sx", "sy"), P("tm", None, "sx", "sy")),
        check_vma=False,
    )
```

```python
import functools

import jax
import jax.numpy as jnp
from jax import lax
from jax.experimental import pallas as pl
from jax.experimental.pallas import tpu as pltpu
from jax.sharding import PartitionSpec as P

RB = 8
FSTEPS = 4
SWEEPS = 3
ITERS = 2
LAYERS = 8
ROWS = 32
COLS = 128
HALO = FSTEPS * SWEEPS
EXT = ROWS + HALO
STRIP = 16
BLOCK = 4

cond_slope = 0.25
joule_slope = 0.3
MESH = pl.DeviceIdType.MESH


def kernel(
    slabs, solvers, chunk,
    state_hbm, decay_hbm, power_hbm, mask_hbm, ids_hbm, cond_hbm,
    out_ref, jump_ref,
    state_ref, decay_ref, power_ref, mask_ref, ids_ref, cond_ref, load_sem,
    own, dec, off, packed, rows_in, side_in, corner_in,
    v, cond, rhs, wx, wy, wz, rden, power, base,
    a_in, b_in, u_out, u_in,
    near_send, near_recv, far_send, far_recv,
):
    tm, sx, sy = lax.axis_index("tm"), lax.axis_index("sx"), lax.axis_index("sy")
    other_core, side, corner = (tm, 1 - sx, sy), (tm, sx, 1 - sy), (tm, 1 - sx, 1 - sy)

    loads = [
        pltpu.make_async_copy(src, dst, load_sem.at[i])
        for i, (src, dst) in enumerate((
            (state_hbm, state_ref), (power_hbm, power_ref), (decay_hbm, decay_ref),
            (ids_hbm, ids_ref), (cond_hbm, cond_ref), (mask_hbm, mask_ref),
        ))
    ]
    for load in loads:
        load.start()

    def slab_at(distance):
        return lax.rem(tm + distance, slabs)

    barrier = pltpu.get_barrier_semaphore()
    for peer in (other_core, side, corner):
        pl.semaphore_signal(barrier, inc=1, device_id=peer, device_id_type=MESH)
    for d in range(1, slabs):
        pl.semaphore_signal(barrier, inc=1, device_id=(slab_at(d), sx, sy), device_id_type=MESH)

    def grid_row(r):
        return r + sx * (ROWS - 1 - 2 * r)

    def grid_block(i):
        return i + sx * (ids_ref.shape[1] - 1 - 2 * i)

    lane = lax.broadcasted_iota(jnp.int32, (LAYERS, COLS), 1)
    window = lax.rem(lane // STRIP + 8, 8)
    edge_window = 7 * (1 - sy)

    def pack(slot, kind, first, last):
        for g in range(first // 8, last // 8):
            total = own[kind, 8 * g] if slot is None else u_in[slot, 8 * g]
            for i in range(1, 8):
                row = own[kind, 8 * g + i] if slot is None else u_in[slot, 8 * g + i]
                here = lax.rem(window - i + 8, 8) == edge_window
                total = jnp.where(here, pltpu.roll(row, STRIP * i, 1), total)
            packed[kind if slot is None else 2, g] = total

    def load_rows(r, carry):
        at = pl.ds(grid_row(r), LAYERS, ROWS)
        own[0, r] = state_ref[at, :]
        own[1, r] = power_ref[at, :]
        dec[r] = decay_ref[at, :]
        return carry

    for load in loads:
        load.wait()
    lax.fori_loop(0, ROWS, load_rows, 0, unroll=True)
    pack(None, 0, 0, ROWS)
    pack(None, 1, 0, ROWS)

    pl.semaphore_wait(barrier, 3 + slabs - 1)

    def near(src_rows, src_strip, src_corner, slots, k):
        copies = [
            pltpu.make_async_remote_copy(
                src_ref=src, dst_ref=dst, send_sem=near_send.at[k + i], recv_sem=near_recv.at[k + i],
                device_id=peer, device_id_type=MESH,
            )
            for i, (src, dst, peer) in enumerate((
                (src_corner, corner_in.at[slots], corner),
                (src_strip, side_in.at[slots], side),
                (src_rows, rows_in.at[slots], other_core),
            ))
        ]
        for copy in copies:
            copy.start()
        return copies

    first = near(
        own.at[:, pl.ds(ROWS - HALO, HALO)], packed.at[pl.ds(0, 2)],
        packed.at[pl.ds(0, 2), pl.ds(2, 2)], pl.ds(0, 2), 0,
    )

    middle = ROWS // 2

    def rows_of(half, t):
        return pl.ds(half * middle + t * chunk, chunk)

    def to_solvers(src, dst, kind, half):
        def copy_at(d):
            target = slab_at(d)
            return pltpu.make_async_remote_copy(
                src_ref=src.at[rows_of(half, target)], dst_ref=dst.at[half, tm],
                send_sem=far_send.at[kind + half, d], recv_sem=far_recv.at[kind + half, d],
                device_id=(target, sx, sy), device_id_type=MESH,
            )

        for d in range(1, slabs):
            guarded(slab_at(d) < solvers, copy_at(d).start)

        def keep():
            dst[half, tm] = src[rows_of(half, tm)]

        guarded(tm < solvers, keep)

        def sent():
            for d in range(1, slabs):
                guarded(slab_at(d) < solvers, copy_at(d).wait_send)

        def arrived():
            for d in range(1, slabs):
                copy_at(d).wait_recv()

        pending.append(sent)
        return lambda: guarded(tm < solvers, arrived)

    def guarded(condition, action):
        if solvers == slabs:
            action()
        else:
            pl.when(condition)(action)

    pending = []
    decay_arrived = [to_solvers(dec, a_in, 0, half) for half in range(2)]

    blank = jnp.zeros((LAYERS, 2 * COLS), jnp.float32)
    for stage in range(HALO + 1):
        v[stage, 0] = blank
    for m in range(FSTEPS):
        cond[m, 0] = blank

    layer = lax.broadcasted_iota(jnp.int32, (LAYERS, 2 * COLS), 0)
    place = lax.broadcasted_iota(jnp.int32, (LAYERS, 2 * COLS), 1)
    for i in range(-(-EXT // RB)):
        block = grid_block(i)
        value = jnp.zeros((LAYERS, 2 * COLS), jnp.float32)
        for l in range(LAYERS):
            value = jnp.where(layer == l, cond_ref[ids_ref[l, block]], value)
        base[i] = value
    first_col = place == sy * COLS
    last_col = place == 2 * COLS - 1 - sy * COLS
    wy_mask = jnp.where(first_col, 0.0, 1.0)
    wz_mask = jnp.where(layer == 0, 0.0, 0.5)
    border = (
        jnp.where(layer == 0, 1.0, 0.0)
        + jnp.where(first_col, 1.0, 0.0)
        + jnp.where(last_col, 1.0, 0.0)
    )

    def spread_side(store, slot):
        for i in range(8):
            for g in range(ROWS // 8):
                store(8 * g + i, 1, pltpu.roll(side_in[slot, g], (COLS - STRIP * i) % COLS, 1))

    def spread_far(store, slot):
        for i in range(HALO):
            store(EXT - 1 - i, 0, rows_in[slot, i])
        for i in range(8):
            for g in range(2):
                r = 2 * ROWS - 1 - (16 + 8 * g + i)
                if r < EXT:
                    store(r, 1, pltpu.roll(corner_in[slot, g], (COLS - STRIP * i) % COLS, 1))

    def store_state(r, half, value):
        v[0, 1 + r, :, half * COLS:(half + 1) * COLS] = value

    def store_power(r, half, value):
        power[1 + r, :, half * COLS:(half + 1) * COLS] = value

    def over(first, last, body):
        full = (last - first) // BLOCK

        def step(i, carry):
            body(first + BLOCK * i, BLOCK)
            return carry

        lax.fori_loop(0, full, step, 0, unroll=True)
        if first + BLOCK * full < last:
            body(first + BLOCK * full, last - first - BLOCK * full)

    def sweep(m, index, first, last):
        source = SWEEPS * m + index

        def body(r, size):
            at, before, after = pl.ds(r + 1, size), pl.ds(r, size), pl.ds(r + 2, size)
            if index == 0:
                k = cond[m, at]
                west = k + cond[m, before]
                east = k + cond[m, after]
                south = wy_mask * (k + pltpu.roll(k, 1, 2))
                down = wz_mask * (k + pltpu.roll(k, 1, 1))
                den = 1.0 + (
                    west + east + south + pltpu.roll(south, 2 * COLS - 1, 2)
                    + down + pltpu.roll(down, LAYERS - 1, 1) + border * k
                )
                guess = pl.reciprocal(den, approx=True)
                inverse = guess * (2.0 - den * guess)
                wx[m, at] = west
                wy[m, at] = south
                wz[m, at] = down
                rden[m, at] = inverse
            else:
                west, east, south = wx[m, at], wx[m, after], wy[m, at]
                down, inverse = wz[m, at], rden[m, at]
            mid = v[source, at]
            total = rhs[m, at] + west * v[source, before] + east * v[source, after]
            total = total + south * pltpu.roll(mid, 1, 2)
            total = total + pltpu.roll(south * mid, 2 * COLS - 1, 2)
            total = total + down * pltpu.roll(mid, 1, 1)
            total = total + pltpu.roll(down * mid, LAYERS - 1, 1)
            total = total * inverse
            if source + 1 < HALO:
                v[source + 1, at] = total
            else:
                v[source + 1, at, :, 0:COLS] = total[:, :, 0:COLS]

        over(first, last, body)

    def prepare(m, first, last):
        coef_now, coef_old, scale = (1.0, 0.0, 1.0) if m == 0 else (4.0 / 3.0, -1.0 / 3.0, 2.0 / 3.0)
        half = 0.5 * scale
        now = SWEEPS * m

        def body(r, size):
            at = pl.ds(r + 1, size)
            block = r // RB
            current = v[now, at]
            t = jnp.tanh(current)
            cond[m, at] = base[block] * (half - (half * cond_slope) * t)
            on = half * mask_ref[0, m, grid_block(block)].astype(jnp.float32)
            total = (on * power[at]) * (1.0 + joule_slope * t)
            if m == 0:
                total = total + current
            else:
                total = total + (coef_now * current + coef_old * v[now - SWEEPS, at])
            rhs[m, at] = total

        aligned = min(-(-first // BLOCK) * BLOCK, last)
        if first < aligned:
            body(first, aligned - first)
        over(aligned, last, body)

    def fine(done, reached):
        for m in range(FSTEPS):
            left = SWEEPS * (FSTEPS - m)
            prepare(m, done + left if done else 0, reached + left)
            for index in range(SWEEPS):
                left -= 1
                sweep(m, index, done + left if done else 0, reached + left)

    def solve(it, half):
        a = [a_in[half, n] for n in range(slabs)]
        total = b_in[it, half, 0]
        product = a[0]
        for n in range(1, slabs):
            total = a[n] * total + b_in[it, half, n]
            product = product * a[n]
        state = total / (1.0 - product)
        for n in range(slabs):
            u_out[it, half, n] = state
            if n < slabs - 1:
                state = a[n] * state + b_in[it, half, n]

    def from_solvers(it, half):
        kind = 2 + 2 * (ITERS + it) + half

        def copy_at(d):
            target = slab_at(d)
            return pltpu.make_async_remote_copy(
                src_ref=u_out.at[it, half, target], dst_ref=u_in.at[it, rows_of(half, tm)],
                send_sem=far_send.at[kind, d], recv_sem=far_recv.at[kind, d],
                device_id=(target, sx, sy), device_id_type=MESH,
            )

        def work():
            solve(it, half)
            for d in range(1, slabs):
                copy_at(d).start()
            u_in[it, rows_of(half, tm)] = u_out[it, half, tm]

        guarded(tm < solvers, work)

        def sent():
            for d in range(1, slabs):
                copy_at(d).wait_send()

        def arrived():
            for d in range(1, slabs):
                guarded(lax.rem(tm - d + slabs, slabs) < solvers, copy_at(d).wait_recv)

        pending.append(lambda: guarded(tm < solvers, sent))
        return arrived

    for r in range(ROWS):
        store_state(r, 0, own[0, r])
        store_power(r, 0, own[1, r])
    corner_copy, side_copy, rows_copy = first
    pending += [copy.wait_send for copy in first]
    side_copy.wait_recv()
    spread_side(store_state, 0)
    spread_side(store_power, 1)

    for it in range(ITERS):
        if it:
            for half in range(2):
                arrived[half]()
                for r in range(half * middle, (half + 1) * middle):
                    store_state(r, 0, u_in[it - 1, r])
                pack(it - 1, 0, half * middle, (half + 1) * middle)
            again = near(
                u_in.at[pl.ds(it - 1, 1), pl.ds(ROWS - HALO, HALO)], packed.at[pl.ds(2, 1)],
                packed.at[pl.ds(2, 1), pl.ds(2, 2)], pl.ds(2, 1), 3,
            )
            corner_copy, side_copy, rows_copy = again
            pending += [copy.wait_send for copy in again]
            side_copy.wait_recv()
            spread_side(store_state, 2)

        def offsets(r, size, it=it):
            at = pl.ds(r, size)
            start = own[0, at] if it == 0 else u_in[it - 1, at]
            off[it, at] = v[HALO, pl.ds(r + 1, size), :, 0:COLS] - dec[at] * start

        fine(0, middle)
        over(0, middle, offsets)
        lower = to_solvers(off.at[it], b_in.at[it], 2 + 2 * it, 0)
        rows_copy.wait_recv()
        corner_copy.wait_recv()
        spread_far(store_state, 2 if it else 0)
        if it == 0:
            spread_far(store_power, 1)
        fine(middle, ROWS)
        over(middle, ROWS, offsets)
        upper = to_solvers(off.at[it], b_in.at[it], 2 + 2 * it, 1)
        if it == 0:
            for wait in decay_arrived:
                wait()
        lower()
        arrived = [from_solvers(it, 0)]
        if it == ITERS - 1:

            def jumps(r, carry, it=it):
                following = dec[r] * u_in[it - 1, r] + off[it - 1, r]
                jump_ref[pl.ds(grid_row(r), LAYERS, ROWS), :] = v[HALO, r + 1, :, 0:COLS] - following
                return carry

            lax.fori_loop(0, ROWS, jumps, 0, unroll=True)
        upper()
        arrived.append(from_solvers(it, 1))

    def finish(r, carry):
        out_ref[pl.ds(grid_row(r), LAYERS, ROWS), :] = u_in[ITERS - 1, r]
        return carry

    for half in range(2):
        arrived[half]()
        lax.fori_loop(half * middle, (half + 1) * middle, finish, 0, unroll=True)
    for wait in pending:
        wait()


def shards(slabs, initial_states, coarse_decay, power_map, power_mask, region_ids, region_conductivity):
    solvers = min(slabs, ROWS // 2)
    chunk = ROWS // 2 // solvers
    flat = (LAYERS * ROWS, COLS)
    f32 = jnp.float32
    tile = (ROWS, LAYERS, COLS)
    wide = (EXT + 2, LAYERS, 2 * COLS)
    steps = (FSTEPS,) + wide
    vmem = pl.BlockSpec(memory_space=pltpu.VMEM)
    anywhere = pl.BlockSpec(memory_space=pl.ANY)
    kinds = 2 + 4 * ITERS
    states, jump = pl.pallas_call(
        functools.partial(kernel, slabs, solvers, chunk),
        out_shape=[jax.ShapeDtypeStruct(flat, f32)] * 2,
        in_specs=[anywhere] * 6,
        out_specs=[vmem] * 2,
        scratch_shapes=[
            *[pltpu.VMEM(flat, f32) for _ in range(3)],
            pltpu.SMEM(power_mask.shape, jnp.int32),
            pltpu.SMEM(region_ids.shape, jnp.int32),
            pltpu.SMEM(region_conductivity.shape, f32),
            pltpu.SemaphoreType.DMA((6,)),
            pltpu.VMEM((2,) + tile, f32),
            pltpu.VMEM(tile, f32),
            pltpu.VMEM((ITERS,) + tile, f32),
            pltpu.VMEM((3, ROWS // 8, LAYERS, COLS), f32),
            pltpu.VMEM((3, HALO, LAYERS, COLS), f32),
            pltpu.VMEM((3, ROWS // 8, LAYERS, COLS), f32),
            pltpu.VMEM((3, 2, LAYERS, COLS), f32),
            pltpu.VMEM((HALO + 1,) + wide, f32),
            *[pltpu.VMEM(steps, f32) for _ in range(6)],
            pltpu.VMEM(wide, f32),
            pltpu.VMEM((-(-EXT // RB), LAYERS, 2 * COLS), f32),
            pltpu.VMEM((2, slabs, chunk, LAYERS, COLS), f32),
            pltpu.VMEM((ITERS, 2, slabs, chunk, LAYERS, COLS), f32),
            pltpu.VMEM((ITERS, 2, slabs, chunk, LAYERS, COLS), f32),
            pltpu.VMEM((ITERS,) + tile, f32),
            pltpu.SemaphoreType.DMA((6,)),
            pltpu.SemaphoreType.DMA((6,)),
            pltpu.SemaphoreType.DMA((kinds, slabs)),
            pltpu.SemaphoreType.DMA((kinds, slabs)),
        ],
        compiler_params=pltpu.CompilerParams(
            collective_id=0, has_side_effects=True, vmem_limit_bytes=56 * 2**20
        ),
    )(
        initial_states.reshape(flat), coarse_decay.reshape(flat), power_map.reshape(flat),
        power_mask, region_ids, region_conductivity,
    )
    return states.reshape(initial_states.shape), jump.reshape(initial_states.shape)


def solution(mesh):
    return jax.shard_map(
        functools.partial(shards, mesh.shape["tm"]),
        mesh=mesh,
        in_specs=(
            P("tm", None, "sx", "sy"),
            P("tm", None, "sx", "sy"),
            P(None, "sx", "sy"),
            P("tm", None, None),
            P(),
            P(),
        ),
        out_specs=(P("tm", None, "sx", "sy"), P("tm", None, "sx", "sy")),
        check_vma=False,
    )
```

```python
import functools

import jax
import jax.numpy as jnp
from jax import lax
from jax.experimental import pallas as pl
from jax.experimental.pallas import tpu as pltpu
from jax.sharding import PartitionSpec as P

RB = 8
FSTEPS = 4
SWEEPS = 3
ITERS = 2
LAYERS = 8
ROWS = 32
COLS = 128
HALO = FSTEPS * SWEEPS
EXT = ROWS + HALO
STRIP = 16
BLOCK = 4

cond_slope = 0.25
joule_slope = 0.3
MESH = pl.DeviceIdType.MESH


def kernel(
    slabs, solvers, chunk,
    state_hbm, decay_hbm, power_hbm, mask_hbm, ids_hbm, cond_hbm,
    out_ref, jump_ref,
    state_ref, decay_ref, power_ref, mask_ref, ids_ref, cond_ref, load_sem,
    own, dec, off, packed, rows_in, side_in, corner_in,
    v, cond, rhs, wx, wy, wz, rden, power, base,
    a_in, b_in, u_out, u_in,
    near_send, near_recv, far_send, far_recv,
):
    tm, sx, sy = lax.axis_index("tm"), lax.axis_index("sx"), lax.axis_index("sy")
    other_core, side, corner = (tm, 1 - sx, sy), (tm, sx, 1 - sy), (tm, 1 - sx, 1 - sy)

    loads = [
        pltpu.make_async_copy(src, dst, load_sem.at[i])
        for i, (src, dst) in enumerate((
            (state_hbm, state_ref), (power_hbm, power_ref), (decay_hbm, decay_ref),
            (ids_hbm, ids_ref), (cond_hbm, cond_ref), (mask_hbm, mask_ref),
        ))
    ]
    for load in loads:
        load.start()

    def slab_at(distance):
        return lax.rem(tm + distance, slabs)

    barrier = pltpu.get_barrier_semaphore()
    for peer in (other_core, side, corner):
        pl.semaphore_signal(barrier, inc=1, device_id=peer, device_id_type=MESH)
    for d in range(1, slabs):
        pl.semaphore_signal(barrier, inc=1, device_id=(slab_at(d), sx, sy), device_id_type=MESH)

    def grid_row(r):
        return r + sx * (ROWS - 1 - 2 * r)

    def grid_block(i):
        return i + sx * (ids_ref.shape[1] - 1 - 2 * i)

    lane = lax.broadcasted_iota(jnp.int32, (LAYERS, COLS), 1)
    window = lax.rem(lane // STRIP + 8, 8)
    edge_window = 7 * (1 - sy)

    def pack(slot, kind):
        for g in range(ROWS // 8):
            total = own[kind, 8 * g] if slot is None else u_in[slot, 8 * g]
            for i in range(1, 8):
                row = own[kind, 8 * g + i] if slot is None else u_in[slot, 8 * g + i]
                here = lax.rem(window - i + 8, 8) == edge_window
                total = jnp.where(here, pltpu.roll(row, STRIP * i, 1), total)
            packed[kind if slot is None else 2, g] = total

    def load_rows(r, carry):
        at = pl.ds(grid_row(r), LAYERS, ROWS)
        own[0, r] = state_ref[at, :]
        own[1, r] = power_ref[at, :]
        dec[r] = decay_ref[at, :]
        return carry

    for load in loads:
        load.wait()
    lax.fori_loop(0, ROWS, load_rows, 0, unroll=True)
    pack(None, 0)
    pack(None, 1)

    pl.semaphore_wait(barrier, 3 + slabs - 1)

    def near(src_rows, src_strip, src_corner, slots, k):
        copies = [
            pltpu.make_async_remote_copy(
                src_ref=src, dst_ref=dst, send_sem=near_send.at[k + i], recv_sem=near_recv.at[k + i],
                device_id=peer, device_id_type=MESH,
            )
            for i, (src, dst, peer) in enumerate((
                (src_corner, corner_in.at[slots], corner),
                (src_strip, side_in.at[slots], side),
                (src_rows, rows_in.at[slots], other_core),
            ))
        ]
        for copy in copies:
            copy.start()
        return copies

    first = near(
        own.at[:, pl.ds(ROWS - HALO, HALO)], packed.at[pl.ds(0, 2)],
        packed.at[pl.ds(0, 2), pl.ds(2, 2)], pl.ds(0, 2), 0,
    )

    def chunk_of(t):
        return t // 2 + (solvers // 2) * lax.rem(t + t // 2, 2)

    def rows_of(t):
        return pl.ds(chunk_of(t) * chunk, chunk)

    def to_solvers(src, dst, kind):
        def copy_at(d):
            target = slab_at(d)
            return pltpu.make_async_remote_copy(
                src_ref=src.at[rows_of(target)], dst_ref=dst.at[tm],
                send_sem=far_send.at[kind, d], recv_sem=far_recv.at[kind, d],
                device_id=(target, sx, sy), device_id_type=MESH,
            )

        def send(half):
            for d in range(1, slabs):
                target = slab_at(d)
                mine = chunk_of(target) // (solvers // 2) == half
                pl.when(mine & (target < solvers))(copy_at(d).start)

        def keep():
            def store():
                dst[tm] = src[rows_of(tm)]

            guarded(tm < solvers, store)

        def sent():
            for d in range(1, slabs):
                guarded(slab_at(d) < solvers, copy_at(d).wait_send)

        def arrived():
            for d in range(1, slabs):
                copy_at(d).wait_recv()

        return send, keep, sent, arrived

    def guarded(condition, action):
        if solvers == slabs:
            action()
        else:
            pl.when(condition)(action)

    send, keep, decay_sent, decay_arrived = to_solvers(dec, a_in, 0)
    send(0)
    send(1)
    keep()

    blank = jnp.zeros((LAYERS, 2 * COLS), jnp.float32)
    for stage in range(HALO + 1):
        v[stage, 0] = blank
    for m in range(FSTEPS):
        cond[m, 0] = blank

    layer = lax.broadcasted_iota(jnp.int32, (LAYERS, 2 * COLS), 0)
    place = lax.broadcasted_iota(jnp.int32, (LAYERS, 2 * COLS), 1)
    for i in range(-(-EXT // RB)):
        block = grid_block(i)
        value = jnp.zeros((LAYERS, 2 * COLS), jnp.float32)
        for l in range(LAYERS):
            value = jnp.where(layer == l, cond_ref[ids_ref[l, block]], value)
        base[i] = value
    first_col = place == sy * COLS
    last_col = place == 2 * COLS - 1 - sy * COLS
    wy_mask = jnp.where(first_col, 0.0, 1.0)
    wz_mask = jnp.where(layer == 0, 0.0, 0.5)
    border = (
        jnp.where(layer == 0, 1.0, 0.0)
        + jnp.where(first_col, 1.0, 0.0)
        + jnp.where(last_col, 1.0, 0.0)
    )

    def spread_side(store, slot):
        for i in range(8):
            for g in range(ROWS // 8):
                store(8 * g + i, 1, pltpu.roll(side_in[slot, g], (COLS - STRIP * i) % COLS, 1))

    def spread_far(store, slot):
        for i in range(HALO):
            store(EXT - 1 - i, 0, rows_in[slot, i])
        for i in range(8):
            for g in range(2):
                r = 2 * ROWS - 1 - (16 + 8 * g + i)
                if r < EXT:
                    store(r, 1, pltpu.roll(corner_in[slot, g], (COLS - STRIP * i) % COLS, 1))

    def store_state(r, half, value):
        v[0, 1 + r, :, half * COLS:(half + 1) * COLS] = value

    def store_power(r, half, value):
        power[1 + r, :, half * COLS:(half + 1) * COLS] = value

    def over(first, last, body):
        full = (last - first) // BLOCK

        def step(i, carry):
            body(first + BLOCK * i, BLOCK)
            return carry

        lax.fori_loop(0, full, step, 0, unroll=True)
        if first + BLOCK * full < last:
            body(first + BLOCK * full, last - first - BLOCK * full)

    def sweep(m, index, first, last):
        source = SWEEPS * m + index

        def body(r, size):
            at, before, after = pl.ds(r + 1, size), pl.ds(r, size), pl.ds(r + 2, size)
            if index == 0:
                k = cond[m, at]
                west = k + cond[m, before]
                east = k + cond[m, after]
                south = wy_mask * (k + pltpu.roll(k, 1, 2))
                down = wz_mask * (k + pltpu.roll(k, 1, 1))
                den = 1.0 + (
                    west + east + south + pltpu.roll(south, 2 * COLS - 1, 2)
                    + down + pltpu.roll(down, LAYERS - 1, 1) + border * k
                )
                guess = pl.reciprocal(den, approx=True)
                inverse = guess * (2.0 - den * guess)
                wx[m, at] = west
                wy[m, at] = south
                wz[m, at] = down
                rden[m, at] = inverse
            else:
                west, east, south = wx[m, at], wx[m, after], wy[m, at]
                down, inverse = wz[m, at], rden[m, at]
            mid = v[source, at]
            total = rhs[m, at] + west * v[source, before] + east * v[source, after]
            total = total + south * pltpu.roll(mid, 1, 2)
            total = total + pltpu.roll(south * mid, 2 * COLS - 1, 2)
            total = total + down * pltpu.roll(mid, 1, 1)
            total = total + pltpu.roll(down * mid, LAYERS - 1, 1)
            total = total * inverse
            if source + 1 < HALO:
                v[source + 1, at] = total
            else:
                v[source + 1, at, :, 0:COLS] = total[:, :, 0:COLS]

        over(first, last, body)

    def prepare(m, first, last):
        coef_now, coef_old, scale = (1.0, 0.0, 1.0) if m == 0 else (4.0 / 3.0, -1.0 / 3.0, 2.0 / 3.0)
        half = 0.5 * scale
        now = SWEEPS * m

        def body(r, size):
            at = pl.ds(r + 1, size)
            block = r // RB
            current = v[now, at]
            t = jnp.tanh(current)
            cond[m, at] = base[block] * (half - (half * cond_slope) * t)
            on = half * mask_ref[0, m, grid_block(block)].astype(jnp.float32)
            total = (on * power[at]) * (1.0 + joule_slope * t)
            if m == 0:
                total = total + current
            else:
                total = total + (coef_now * current + coef_old * v[now - SWEEPS, at])
            rhs[m, at] = total

        aligned = min(-(-first // BLOCK) * BLOCK, last)
        if first < aligned:
            body(first, aligned - first)
        over(aligned, last, body)

    def fine(done, reached):
        for m in range(FSTEPS):
            left = SWEEPS * (FSTEPS - m)
            prepare(m, done + left if done else 0, reached + left)
            for index in range(SWEEPS):
                left -= 1
                sweep(m, index, done + left if done else 0, reached + left)

    def solve(it):
        a = [a_in[n] for n in range(slabs)]
        total = b_in[it, 0]
        product = a[0]
        for n in range(1, slabs):
            total = a[n] * total + b_in[it, n]
            product = product * a[n]
        state = total / (1.0 - product)
        for n in range(slabs):
            u_out[it, n] = state
            if n < slabs - 1:
                state = a[n] * state + b_in[it, n]

    def from_solvers(it):
        kind = 1 + ITERS + it

        def copy_at(d):
            target = slab_at(d)
            return pltpu.make_async_remote_copy(
                src_ref=u_out.at[it, target], dst_ref=u_in.at[it, rows_of(tm)],
                send_sem=far_send.at[kind, d], recv_sem=far_recv.at[kind, d],
                device_id=(target, sx, sy), device_id_type=MESH,
            )

        def work():
            solve(it)
            for d in range(1, slabs):
                copy_at(d).start()
            u_in[it, rows_of(tm)] = u_out[it, tm]

        guarded(tm < solvers, work)

        def sent():
            for d in range(1, slabs):
                copy_at(d).wait_send()

        def arrived():
            for d in range(1, slabs):
                guarded(lax.rem(tm - d + slabs, slabs) < solvers, copy_at(d).wait_recv)

        return lambda: guarded(tm < solvers, sent), arrived

    pending = [decay_sent]
    for r in range(ROWS):
        store_state(r, 0, own[0, r])
        store_power(r, 0, own[1, r])
    corner_copy, side_copy, rows_copy = first
    pending += [copy.wait_send for copy in first]
    side_copy.wait_recv()
    spread_side(store_state, 0)
    spread_side(store_power, 1)

    for it in range(ITERS):
        if it:
            pack(it - 1, 0)
            again = near(
                u_in.at[pl.ds(it - 1, 1), pl.ds(ROWS - HALO, HALO)], packed.at[pl.ds(2, 1)],
                packed.at[pl.ds(2, 1), pl.ds(2, 2)], pl.ds(2, 1), 3,
            )
            corner_copy, side_copy, rows_copy = again
            pending += [copy.wait_send for copy in again]
            for r in range(ROWS):
                store_state(r, 0, u_in[it - 1, r])
            side_copy.wait_recv()
            spread_side(store_state, 2)
        send, keep, sent, arrived = to_solvers(off.at[it], b_in.at[it], 1 + it)

        def offsets(r, size, it=it):
            at = pl.ds(r, size)
            start = own[0, at] if it == 0 else u_in[it - 1, at]
            off[it, at] = v[HALO, pl.ds(r + 1, size), :, 0:COLS] - dec[at] * start

        middle = ROWS // 2
        fine(0, middle)
        over(0, middle, offsets)
        send(0)
        rows_copy.wait_recv()
        corner_copy.wait_recv()
        spread_far(store_state, 2 if it else 0)
        if it == 0:
            spread_far(store_power, 1)
        fine(middle, ROWS)
        over(middle, ROWS, offsets)
        send(1)
        keep()
        pending.append(sent)
        if it == 0:
            guarded(tm < solvers, decay_arrived)
        if it == ITERS - 1:

            def jumps(r, carry, it=it):
                following = dec[r] * u_in[it - 1, r] + off[it - 1, r]
                jump_ref[pl.ds(grid_row(r), LAYERS, ROWS), :] = v[HALO, r + 1, :, 0:COLS] - following
                return carry

            lax.fori_loop(0, ROWS, jumps, 0, unroll=True)
        guarded(tm < solvers, arrived)
        sent, arrived = from_solvers(it)
        pending.append(sent)
        arrived()

    def finish(r, carry):
        out_ref[pl.ds(grid_row(r), LAYERS, ROWS), :] = u_in[ITERS - 1, r]
        return carry

    lax.fori_loop(0, ROWS, finish, 0, unroll=True)
    for wait in pending:
        wait()


def shards(slabs, initial_states, coarse_decay, power_map, power_mask, region_ids, region_conductivity):
    solvers = min(slabs, ROWS)
    chunk = ROWS // solvers
    flat = (LAYERS * ROWS, COLS)
    f32 = jnp.float32
    tile = (ROWS, LAYERS, COLS)
    wide = (EXT + 2, LAYERS, 2 * COLS)
    steps = (FSTEPS,) + wide
    vmem = pl.BlockSpec(memory_space=pltpu.VMEM)
    anywhere = pl.BlockSpec(memory_space=pl.ANY)
    kinds = 1 + 2 * ITERS
    states, jump = pl.pallas_call(
        functools.partial(kernel, slabs, solvers, chunk),
        out_shape=[jax.ShapeDtypeStruct(flat, f32)] * 2,
        in_specs=[anywhere] * 6,
        out_specs=[vmem] * 2,
        scratch_shapes=[
            *[pltpu.VMEM(flat, f32) for _ in range(3)],
            pltpu.SMEM(power_mask.shape, jnp.int32),
            pltpu.SMEM(region_ids.shape, jnp.int32),
            pltpu.SMEM(region_conductivity.shape, f32),
            pltpu.SemaphoreType.DMA((6,)),
            pltpu.VMEM((2,) + tile, f32),
            pltpu.VMEM(tile, f32),
            pltpu.VMEM((ITERS,) + tile, f32),
            pltpu.VMEM((3, ROWS // 8, LAYERS, COLS), f32),
            pltpu.VMEM((3, HALO, LAYERS, COLS), f32),
            pltpu.VMEM((3, ROWS // 8, LAYERS, COLS), f32),
            pltpu.VMEM((3, 2, LAYERS, COLS), f32),
            pltpu.VMEM((HALO + 1,) + wide, f32),
            *[pltpu.VMEM(steps, f32) for _ in range(6)],
            pltpu.VMEM(wide, f32),
            pltpu.VMEM((-(-EXT // RB), LAYERS, 2 * COLS), f32),
            pltpu.VMEM((slabs, chunk, LAYERS, COLS), f32),
            pltpu.VMEM((ITERS, slabs, chunk, LAYERS, COLS), f32),
            pltpu.VMEM((ITERS, slabs, chunk, LAYERS, COLS), f32),
            pltpu.VMEM((ITERS,) + tile, f32),
            pltpu.SemaphoreType.DMA((6,)),
            pltpu.SemaphoreType.DMA((6,)),
            pltpu.SemaphoreType.DMA((kinds, slabs)),
            pltpu.SemaphoreType.DMA((kinds, slabs)),
        ],
        compiler_params=pltpu.CompilerParams(
            collective_id=0, has_side_effects=True, vmem_limit_bytes=56 * 2**20
        ),
    )(
        initial_states.reshape(flat), coarse_decay.reshape(flat), power_map.reshape(flat),
        power_mask, region_ids, region_conductivity,
    )
    return states.reshape(initial_states.shape), jump.reshape(initial_states.shape)


def solution(mesh):
    return jax.shard_map(
        functools.partial(shards, mesh.shape["tm"]),
        mesh=mesh,
        in_specs=(
            P("tm", None, "sx", "sy"),
            P("tm", None, "sx", "sy"),
            P(None, "sx", "sy"),
            P("tm", None, None),
            P(),
            P(),
        ),
        out_specs=(P("tm", None, "sx", "sy"), P("tm", None, "sx", "sy")),
        check_vma=False,
    )
```
